32 devices in a mesh: section: 2 (over y), dp: 4 (over x, core), mp: 4 (over z).
Axes of the slice: x: 2, y: 2, z: 4, core: 2. Of those that a mesh axis runs over, the one named last changes fastest.
Arguments:
- activations: bfloat16 [768, 27648], P(('dp', 'section'), 'mp'), may hold values from -6 to 6
- weight: bfloat16 [27648, 5120], P('mp', 'section'), may hold values from -0.0390625 to 0.0390625
- readout: bfloat16 [768, 5120], P('dp', 'section'), may hold values from -0.02734375 to 0.02734375
- logp_rest: float32 [768], P('dp'), may hold values from -1.2 to 1.2
- old_logp: float32 [768], P('dp'), may hold values from -1.2 to 1.2
- ref_logp: float32 [768], P('dp'), may hold values from -4 to 4
- lengths: int32 [2], replicated, may hold values from 1 to 384, as said below
- group_ids: int32 [2], replicated, may hold values from 0 to 0, as said below
- rewards: float32 [2], replicated, may hold values from -6 to 6
- first_moment: float32 [4, 6912, 5120], P('mp', 'dp', 'section'), may hold values from -0.0006 to 0.0006
- second_moment: float32 [4, 6912, 5120], P('mp', 'dp', 'section'), may hold values from 1e-10 to 1e-05
Outputs:
- new_weight: bfloat16 [27648, 5120], P('mp', 'section')
- new_first: float32 [4, 6912, 5120], P('mp', 'dp', 'section')
- new_second: float32 [4, 6912, 5120], P('mp', 'dp', 'section')
The draws below stay inside these ranges and needn't reach their ends.
Inputs may be any that keep to these rules, and one draw needn't show every extreme that they name: `lengths`: every response has at least one live token, and some response has all 384 slots live. `group_ids`: each group id names exactly 2 responses.
All inputs are finite; a program needn't handle non-finite values.
Results may differ from the reference program's by a relative error of at most 0.015.
Values may be sent and summed in bfloat16 or wider, within the bound.
A program may use at most 256 MiB of HBM per device.

```python
import math
import jax
import jax.numpy as jnp
from jax import lax

D = 5120
FF = 27648
RESP_LEN = 384
GROUP = 2
TOK_REP = 192
TOKENS = 768
RESP = 2
N_DP = 4
N_MP = 4


def draw_lengths(key, part):
    first_key, second_key = jax.random.split(jax.random.fold_in(key, 11))
    drawn = jax.random.randint(first_key, (RESP,), 1, RESP_LEN + 1)
    longest = jax.random.randint(second_key, (), 0, RESP)
    return jnp.where(jnp.arange(RESP) == longest, RESP_LEN, drawn).astype(jnp.int32)


def draw_group_ids(key, part):
    shuffled = jax.random.permutation(jax.random.fold_in(key, 23), RESP)
    return (shuffled // GROUP).astype(jnp.int32)


def levels(stream_key, extent, cuts, least, top_value):
    factor_of = 1.0
    for dim, parts in cuts:
        draws = jax.random.uniform(jax.random.fold_in(jax.random.fold_in(stream_key, 6), dim), (parts,), jnp.float32, least / len(cuts), top_value / len(cuts))
        factor_of = factor_of * jnp.repeat(jnp.exp(draws), extent[dim] // parts).reshape((-1,) + (1,) * (len(extent) - 1 - dim))
    return factor_of


def normal_values(own_key, dims, spread, reach, pieces=(), held_as=jnp.bfloat16):
    values = spread * jax.random.normal(own_key, dims, jnp.float32)
    if pieces:
        values = values * levels(own_key, dims, pieces, -0.22, 0.18)
    return jnp.clip(values, -reach, reach).astype(held_as)


def setup_inputs(seed: int = 0) -> dict:
    keys = jax.random.split(jax.random.key(seed), 12)
    activations = normal_values(keys[0], (TOKENS, FF), 1.0, 6.0, ((0, 8), (1, 4)))
    weight = normal_values(keys[1], (FF, D), FF ** -0.5, 0.0390625, ((0, 4), (1, 2)))
    readout = normal_values(keys[2], (TOKENS, D), (D * 11) ** -0.5, 0.02734375, ((0, 4), (1, 2)))
    logp_rest = normal_values(keys[3], (TOKENS,), 0.2, 1.2, ((0, 4),), jnp.float32)
    old_logp = normal_values(keys[4], (TOKENS,), 0.2, 1.2, ((0, 4),), jnp.float32)
    ref_logp = normal_values(keys[5], (TOKENS,), 0.8, 4.0, ((0, 4),), jnp.float32)
    lengths = draw_lengths(jax.random.fold_in(keys[11], 71), 0)
    group_ids = draw_group_ids(jax.random.fold_in(keys[11], 71), 0)
    rewards = normal_values(keys[8], (RESP,), 1.5, 6.0, (), jnp.float32)
    first_moment = normal_values(keys[9], (N_MP, FF // N_MP, D), 0.0001, 0.0006, ((0, 4), (1, 4), (2, 2)), jnp.float32)
    second_moment = jnp.clip(jnp.exp(math.log(9.999999747378752e-06) - 11.512925 * jax.random.uniform(keys[10], (N_MP, FF // N_MP, D), jnp.float32) ** levels(keys[10], (N_MP, FF // N_MP, D), ((0, 4), (1, 4), (2, 2)), -0.2, 0.2)), 1.000000013351432e-10, 9.999999747378752e-06)
    return dict(activations=activations, weight=weight, readout=readout, logp_rest=logp_rest, old_logp=old_logp, ref_logp=ref_logp, lengths=lengths, group_ids=group_ids, rewards=rewards, first_moment=first_moment, second_moment=second_moment)


clip_eps = 0.2
kl_coef = 0.1
beta_one = 0.9
beta_two = 0.95
adam_eps = 1e-08
learn_rate = 0.0003
weight_decay = 0.1
first_correct = 1.0 - 0.9 ** 10
second_correct = 1.0 - 0.95 ** 10

def token_terms(lengths, group_ids, rewards, positions, resp_len):
    total_resp = rewards.shape[0]
    members = (group_ids[:, None] == group_ids[None, :]).astype(jnp.float32)
    group_size = lax.optimization_barrier(jnp.sum(members, axis=1))
    group_mean = lax.optimization_barrier(jnp.sum(members * rewards[None, :], axis=1)) / group_size
    deviation = rewards[None, :] - group_mean[:, None]
    group_spread = jnp.sqrt(lax.optimization_barrier(jnp.sum(members * deviation * deviation, axis=1)) / group_size)
    advantage = (rewards - group_mean) / jnp.maximum(group_spread, 1.0)
    response = positions // resp_len
    slot_index = (positions % resp_len).astype(jnp.float32)
    picker = (response[:, None] == jnp.arange(total_resp, dtype=jnp.int32)[None, :]).astype(jnp.float32)
    adv_token = lax.optimization_barrier(jnp.sum(picker * advantage[None, :], axis=1))
    len_token = lax.optimization_barrier(jnp.sum(picker * lengths.astype(jnp.float32)[None, :], axis=1))
    token_weight = jnp.where(slot_index < len_token, 1.0 / (len_token * total_resp), 0.0)
    return (adv_token, token_weight)

def token_loss(new_logp, old_logp, ref_logp, adv_token, token_weight):
    ratio = jnp.exp(new_logp - old_logp)
    surrogate = jnp.minimum(ratio * adv_token, jnp.clip(ratio, 1.0 - clip_eps, 1.0 + clip_eps) * adv_token)
    gap = ref_logp - new_logp
    kl_term = jnp.exp(gap) - gap - 1.0
    return jnp.sum(token_weight * (kl_coef * kl_term - surrogate))

def token_coeff(new_logp, old_logp, ref_logp, adv_token, token_weight):

    def loss_of(values):
        return token_loss(values, old_logp, ref_logp, adv_token, token_weight)
    _, pullback = jax.vjp(loss_of, new_logp)
    return pullback(jnp.float32(1.0))[0]

def adam_rows(weight_rows, first_rows, second_rows, gradient):
    new_first = beta_one * first_rows + (1.0 - beta_one) * gradient
    new_second = beta_two * second_rows + (1.0 - beta_two) * gradient * gradient
    current = weight_rows.astype(jnp.float32)
    update = new_first / first_correct / (jnp.sqrt(new_second / second_correct) + adam_eps) + weight_decay * current
    return ((current - learn_rate * update).astype(jnp.bfloat16), new_first, new_second)

def reference(activations, weight, readout, logp_rest, old_logp, ref_logp, lengths, group_ids, rewards, first_moment, second_moment):
    layer_out = jnp.dot(activations, weight, preferred_element_type=jnp.float32)
    score = lax.optimization_barrier(jnp.sum(layer_out * readout.astype(jnp.float32), axis=1))
    new_logp = logp_rest + score
    positions = jnp.arange(TOKENS, dtype=jnp.int32)
    adv_token, token_weight = token_terms(lengths, group_ids, rewards, positions, RESP_LEN)
    coeff = token_coeff(new_logp, old_logp, ref_logp, adv_token, token_weight)
    weighted = (coeff[:, None] * readout.astype(jnp.float32)).astype(jnp.bfloat16)
    act_blocks = activations.reshape(N_DP, TOK_REP, FF)
    weighted_blocks = weighted.reshape(N_DP, TOK_REP, D)

    def add_replica(total, pair):
        part = lax.dot_general(pair[0], pair[1], (((0,), (0,)), ((), ())), preferred_element_type=jnp.float32)
        return (total + part.astype(jnp.bfloat16).astype(jnp.float32), None)
    gradient, _ = lax.scan(add_replica, jnp.zeros((FF, D), jnp.float32), (act_blocks, weighted_blocks))
    first_flat = first_moment.reshape(FF, D)
    second_flat = second_moment.reshape(FF, D)
    new_weight, new_first, new_second = adam_rows(weight, first_flat, second_flat, gradient)
    return (new_weight, new_first.reshape(N_MP, FF // N_MP, D), new_second.reshape(N_MP, FF // N_MP, D))
```

```python
import functools

import jax
import jax.numpy as jnp
from jax import lax
from jax.experimental import pallas as pl
from jax.experimental.pallas import tpu as pltpu
from jax.sharding import PartitionSpec as P

RESP_LEN = 384


clip_eps = 0.2
kl_coef = 0.1
beta_one = 0.9
beta_two = 0.95
adam_eps = 1e-08
learn_rate = 0.0003
weight_decay = 0.1
first_correct = 1.0 - 0.9**10
second_correct = 1.0 - 0.95**10


def token_terms(lengths, group_ids, rewards, positions, resp_len):
    total_resp = rewards.shape[0]
    members = (group_ids[:, None] == group_ids[None, :]).astype(jnp.float32)
    group_size = jnp.sum(members, axis=1)
    group_mean = jnp.sum(members * rewards[None, :], axis=1) / group_size
    deviation = rewards[None, :] - group_mean[:, None]
    group_spread = jnp.sqrt(jnp.sum(members * deviation * deviation, axis=1) / group_size)
    advantage = (rewards - group_mean) / jnp.maximum(group_spread, 1.0)
    response = positions // resp_len
    slot_index = (positions % resp_len).astype(jnp.float32)
    picker = (response[:, None] == jnp.arange(total_resp, dtype=jnp.int32)[None, :]).astype(
        jnp.float32
    )
    adv_token = jnp.sum(picker * advantage[None, :], axis=1)
    len_token = jnp.sum(picker * lengths.astype(jnp.float32)[None, :], axis=1)
    token_weight = jnp.where(slot_index < len_token, 1.0 / (len_token * total_resp), 0.0)
    return (adv_token, token_weight)


def token_loss(new_logp, old_logp, ref_logp, adv_token, token_weight):
    ratio = jnp.exp(new_logp - old_logp)
    surrogate = jnp.minimum(
        ratio * adv_token, jnp.clip(ratio, 1.0 - clip_eps, 1.0 + clip_eps) * adv_token
    )
    gap = ref_logp - new_logp
    kl_term = jnp.exp(gap) - gap - 1.0
    return jnp.sum(token_weight * (kl_coef * kl_term - surrogate))


def token_coeff(new_logp, old_logp, ref_logp, adv_token, token_weight):

    def loss_of(values):
        return token_loss(values, old_logp, ref_logp, adv_token, token_weight)

    _, pullback = jax.vjp(loss_of, new_logp)
    return pullback(jnp.float32(1.0))[0]


def adam_rows(weight_rows, first_rows, second_rows, gradient):
    new_first = beta_one * first_rows + (1.0 - beta_one) * gradient
    new_second = beta_two * second_rows + (1.0 - beta_two) * gradient * gradient
    current = weight_rows.astype(jnp.float32)
    update = (
        new_first / first_correct / (jnp.sqrt(new_second / second_correct) + adam_eps)
        + weight_decay * current
    )
    return ((current - learn_rate * update).astype(jnp.bfloat16), new_first, new_second)


def update_kernel(place, left, right, weight, first, second, *rest):
    updated, new_first, new_second = rest[-3:]
    gradient = jnp.dot(left[...], right[...], preferred_element_type=jnp.float32)
    updated[...], new_first[...], new_second[...] = adam_rows(
        weight[...], first[...], second[...], gradient
    )


def update_rows(place, left, right, weight, first, second, carried, start, rows, tile):
    columns = weight.shape[1]
    tokens = right.shape[0]
    tiles = rows // tile
    begin = start // tile
    shard_tiles = first.shape[0] // tile
    here = lambda i, place: (begin + i, 0)
    moment = pl.BlockSpec((tile, columns), here)
    in_specs = [
        pl.BlockSpec((tile, tokens), here),
        pl.BlockSpec((tokens, columns), lambda i, place: (0, 0)),
        pl.BlockSpec((tile, columns), lambda i, place: (place[0] * shard_tiles + begin + i, 0)),
        moment,
        moment,
    ]
    operands = [left, right, weight, first, second]
    aliases = {}
    if carried is not None:
        in_specs += [pl.BlockSpec(memory_space=pl.ANY)] * 2
        operands += list(carried)
        aliases = {6: 1, 7: 2}
    return pl.pallas_call(
        update_kernel,
        grid_spec=pltpu.PrefetchScalarGridSpec(
            num_scalar_prefetch=1,
            grid=(tiles,),
            in_specs=in_specs,
            out_specs=[pl.BlockSpec((tile, columns), lambda i, place: (i, 0)), moment, moment],
        ),
        out_shape=[
            jax.ShapeDtypeStruct((rows, columns), jnp.bfloat16),
            jax.ShapeDtypeStruct(first.shape, jnp.float32),
            jax.ShapeDtypeStruct(second.shape, jnp.float32),
        ],
        input_output_aliases=aliases,
        compiler_params=pltpu.CompilerParams(vmem_limit_bytes=40 * 2**20),
        cost_estimate=pl.CostEstimate(
            flops=2 * rows * tokens * columns,
            bytes_accessed=20 * rows * columns,
            transcendentals=rows * columns,
        ),
    )(place, *operands)


def place_kernel(count, shard_rows, start, owners, *rest):
    pieces = rest[:count]
    sems = rest[-1]
    whole = rest[-2]
    rows = pieces[0].shape[0]
    copies = []
    for i in range(count):
        row = pl.multiple_of(owners[i] * shard_rows + start, 16)
        copies.append(pltpu.make_async_copy(pieces[i], whole.at[pl.ds(row, rows)], sems.at[i]))
    for copy in copies:
        copy.start()
    for copy in copies:
        copy.wait()


def place_rows(owners, pieces, carried, shard_rows, start):
    count = len(pieces)
    rows, columns = pieces[0].shape
    anywhere = pl.BlockSpec(memory_space=pl.ANY)
    operands = list(pieces) + ([] if carried is None else [carried])
    return pl.pallas_call(
        functools.partial(place_kernel, count, shard_rows, start),
        in_specs=[pl.BlockSpec(memory_space=pltpu.SMEM)] + [anywhere] * len(operands),
        out_specs=anywhere,
        out_shape=jax.ShapeDtypeStruct((count * shard_rows, columns), jnp.bfloat16),
        scratch_shapes=[pltpu.SemaphoreType.DMA((count,))],
        input_output_aliases={} if carried is None else {count + 1: 0},
        cost_estimate=pl.CostEstimate(
            flops=0, bytes_accessed=4 * count * rows * columns, transcendentals=0
        ),
    )(owners, *operands)


def spread(chunk, me, count):
    pieces = [(me, chunk)]
    stride = 2 if count % 2 == 0 else 1
    for hop in range(stride, count, stride):
        sent = lax.ppermute(chunk, "dp", [(i, (i + hop) % count) for i in range(count)])
        pieces.append((lax.rem(me - hop + count, count), sent))
    if stride == 2:
        swap = [(i, i ^ 1) for i in range(count)]
        for owner, piece in list(pieces):
            pieces.append((owner ^ 1, lax.ppermute(piece, "dp", swap)))
    return pieces


def on_device(
    activations,
    weight,
    readout,
    logp_rest,
    old_logp,
    ref_logp,
    lengths,
    group_ids,
    rewards,
    first_moment,
    second_moment,
):
    count = lax.axis_size("dp")
    me = lax.axis_index("dp")
    shard_rows = first_moment.shape[1]
    shifts = [[(i, (i + hop) % count) for i in range(count)] for hop in range(1, count)]

    gathered = lax.all_gather(activations, "section", axis=0, tiled=True)
    tok_rep = gathered.shape[0]
    tokens = count * tok_rep
    blocks = gathered.reshape(tok_rep, count, shard_rows)

    def block_for(owner):
        return lax.dynamic_index_in_dim(blocks, owner, axis=1, keepdims=False)

    left = [block_for(me)]
    right = [readout]
    for hop in range(1, count):
        left.append(lax.ppermute(block_for(lax.rem(me + hop, count)), "dp", shifts[hop - 1]))
        right.append(lax.ppermute(readout, "dp", shifts[hop - 1]))
    order = [lax.rem(me - hop + count, count) for hop in range(count)]

    layer_out = jnp.dot(gathered, weight, preferred_element_type=jnp.float32)
    score_share = jnp.sum(layer_out * readout.astype(jnp.float32), axis=1)
    first_holder = (lax.axis_index("section") + lax.axis_index("mp")) == 0
    once = jnp.where(first_holder, 1.0, 0.0).astype(jnp.float32)
    mine = jnp.stack([score_share + once * logp_rest, once * old_logp, once * ref_logp])
    slots = (jnp.arange(count) == me).astype(jnp.float32)
    known = lax.psum(mine[:, None, :] * slots[None, :, None], ("section", "dp", "mp"))
    known = known.reshape(3, tokens)
    positions = jnp.arange(tokens, dtype=jnp.int32)
    adv_token, token_weight = token_terms(lengths, group_ids, rewards, positions, RESP_LEN)
    coeff = token_coeff(known[0], known[1], known[2], adv_token, token_weight)
    coeff = coeff.reshape(count, tok_rep)
    coeff = jnp.concatenate(
        [lax.dynamic_index_in_dim(coeff, owner, axis=0, keepdims=False) for owner in order]
    )

    left = jnp.concatenate(left, axis=0).T
    right = jnp.concatenate(right, axis=0)
    weighted = (coeff[:, None] * right.astype(jnp.float32)).astype(jnp.bfloat16)

    chunks = max(n for n in range(1, 7) if shard_rows % (16 * n) == 0)
    rows = shard_rows // chunks
    tile = rows // 2 if rows % 32 == 0 else rows
    where_am_i = me.reshape(1).astype(jnp.int32)
    moments = None
    sent = []
    for chunk in range(chunks):
        updated, *moments = update_rows(
            where_am_i,
            left,
            weighted,
            weight,
            first_moment[0],
            second_moment[0],
            moments,
            chunk * rows,
            rows,
            tile,
        )
        sent.append(spread(updated, me, count))
    new_weight = None
    for chunk, pieces in enumerate(sent):
        owners = jnp.stack([owner for owner, _ in pieces]).astype(jnp.int32)
        new_weight = place_rows(
            owners, [piece for _, piece in pieces], new_weight, shard_rows, chunk * rows
        )
    return (new_weight, moments[0][None], moments[1][None])


def solution(mesh):
    placed = (
        P(("dp", "section"), "mp"),
        P("mp", "section"),
        P("dp", "section"),
        P("dp"),
        P("dp"),
        P("dp"),
        P(),
        P(),
        P(),
        P("mp", "dp", "section"),
        P("mp", "dp", "section"),
    )
    return jax.shard_map(
        on_device,
        mesh=mesh,
        in_specs=placed,
        out_specs=(P("mp", "section"), P("mp", "dp", "section"), P("mp", "dp", "section")),
        check_vma=False,
    )
```

```python
import functools

import jax
import jax.numpy as jnp
from jax import lax
from jax.experimental import pallas as pl
from jax.experimental.pallas import tpu as pltpu
from jax.sharding import PartitionSpec as P

RESP_LEN = 384


clip_eps = 0.2
kl_coef = 0.1
beta_one = 0.9
beta_two = 0.95
adam_eps = 1e-08
learn_rate = 0.0003
weight_decay = 0.1
first_correct = 1.0 - 0.9**10
second_correct = 1.0 - 0.95**10


def token_terms(lengths, group_ids, rewards, positions, resp_len):
    total_resp = rewards.shape[0]
    members = (group_ids[:, None] == group_ids[None, :]).astype(jnp.float32)
    group_size = jnp.sum(members, axis=1)
    group_mean = jnp.sum(members * rewards[None, :], axis=1) / group_size
    deviation = rewards[None, :] - group_mean[:, None]
    group_spread = jnp.sqrt(jnp.sum(members * deviation * deviation, axis=1) / group_size)
    advantage = (rewards - group_mean) / jnp.maximum(group_spread, 1.0)
    response = positions // resp_len
    slot_index = (positions % resp_len).astype(jnp.float32)
    picker = (response[:, None] == jnp.arange(total_resp, dtype=jnp.int32)[None, :]).astype(
        jnp.float32
    )
    adv_token = jnp.sum(picker * advantage[None, :], axis=1)
    len_token = jnp.sum(picker * lengths.astype(jnp.float32)[None, :], axis=1)
    token_weight = jnp.where(slot_index < len_token, 1.0 / (len_token * total_resp), 0.0)
    return (adv_token, token_weight)


def token_loss(new_logp, old_logp, ref_logp, adv_token, token_weight):
    ratio = jnp.exp(new_logp - old_logp)
    surrogate = jnp.minimum(
        ratio * adv_token, jnp.clip(ratio, 1.0 - clip_eps, 1.0 + clip_eps) * adv_token
    )
    gap = ref_logp - new_logp
    kl_term = jnp.exp(gap) - gap - 1.0
    return jnp.sum(token_weight * (kl_coef * kl_term - surrogate))


def token_coeff(new_logp, old_logp, ref_logp, adv_token, token_weight):

    def loss_of(values):
        return token_loss(values, old_logp, ref_logp, adv_token, token_weight)

    _, pullback = jax.vjp(loss_of, new_logp)
    return pullback(jnp.float32(1.0))[0]


def adam_rows(weight_rows, first_rows, second_rows, gradient):
    new_first = beta_one * first_rows + (1.0 - beta_one) * gradient
    new_second = beta_two * second_rows + (1.0 - beta_two) * gradient * gradient
    current = weight_rows.astype(jnp.float32)
    update = (
        new_first / first_correct / (jnp.sqrt(new_second / second_correct) + adam_eps)
        + weight_decay * current
    )
    return ((current - learn_rate * update).astype(jnp.bfloat16), new_first, new_second)


def update_kernel(place, left, right, weight, first, second, *rest):
    updated, new_first, new_second = rest[-3:]
    gradient = jnp.dot(left[...], right[...], preferred_element_type=jnp.float32)
    updated[...], new_first[...], new_second[...] = adam_rows(
        weight[...], first[...], second[...], gradient
    )


def update_rows(place, left, right, weight, first, second, carried, after, start, rows, tile):
    columns = weight.shape[1]
    tokens = right.shape[0]
    tiles = rows // tile
    begin = start // tile
    shard_tiles = first.shape[0] // tile
    here = lambda i, place: (begin + i, 0)
    moment = pl.BlockSpec((tile, columns), here)
    in_specs = [
        pl.BlockSpec((tile, tokens), here),
        pl.BlockSpec((tokens, columns), lambda i, place: (0, 0)),
        pl.BlockSpec((tile, columns), lambda i, place: (place[0] * shard_tiles + begin + i, 0)),
        moment,
        moment,
    ]
    operands = [left, right, weight, first, second]
    aliases = {}
    if carried is not None:
        in_specs += [pl.BlockSpec(memory_space=pl.ANY)] * 2
        operands += list(carried)
        aliases = {6: 1, 7: 2}
    if after is not None:
        in_specs.append(pl.BlockSpec(memory_space=pl.ANY))
        operands.append(after)
    return pl.pallas_call(
        update_kernel,
        grid_spec=pltpu.PrefetchScalarGridSpec(
            num_scalar_prefetch=1,
            grid=(tiles,),
            in_specs=in_specs,
            out_specs=[pl.BlockSpec((tile, columns), lambda i, place: (i, 0)), moment, moment],
        ),
        out_shape=[
            jax.ShapeDtypeStruct((rows, columns), jnp.bfloat16),
            jax.ShapeDtypeStruct(first.shape, jnp.float32),
            jax.ShapeDtypeStruct(second.shape, jnp.float32),
        ],
        input_output_aliases=aliases,
        compiler_params=pltpu.CompilerParams(vmem_limit_bytes=40 * 2**20),
        cost_estimate=pl.CostEstimate(
            flops=2 * rows * tokens * columns,
            bytes_accessed=20 * rows * columns,
            transcendentals=rows * columns,
        ),
    )(place, *operands)


def place_kernel(count, shard_rows, start, owners, *rest):
    pieces = rest[:count]
    whole, token, held, in_sems, out_sems = rest[-5:]
    rows = pieces[0].shape[0]
    into = [
        pltpu.make_async_copy(pieces[i], held.at[i], in_sems.at[i]) for i in range(count)
    ]
    for copy in into:
        copy.start()
    token[...] = jnp.zeros_like(token)
    out = []
    for i in range(count):
        row = pl.multiple_of(owners[i] * shard_rows + start, 16)
        into[i].wait()
        out.append(pltpu.make_async_copy(held.at[i], whole.at[pl.ds(row, rows)], out_sems.at[i]))
        out[i].start()
    for copy in out:
        copy.wait()


def place_rows(owners, pieces, carried, shard_rows, start):
    count = len(pieces)
    rows, columns = pieces[0].shape
    anywhere = pl.BlockSpec(memory_space=pl.ANY)
    operands = list(pieces) + ([] if carried is None else [carried])
    return pl.pallas_call(
        functools.partial(place_kernel, count, shard_rows, start),
        in_specs=[pl.BlockSpec(memory_space=pltpu.SMEM)] + [anywhere] * len(operands),
        out_specs=[anywhere, pl.BlockSpec(memory_space=pltpu.VMEM)],
        out_shape=[
            jax.ShapeDtypeStruct((count * shard_rows, columns), jnp.bfloat16),
            jax.ShapeDtypeStruct((8, 128), jnp.float32),
        ],
        scratch_shapes=[
            pltpu.VMEM((count, rows, columns), jnp.bfloat16),
            pltpu.SemaphoreType.DMA((count,)),
            pltpu.SemaphoreType.DMA((count,)),
        ],
        input_output_aliases={} if carried is None else {count + 1: 0},
        compiler_params=pltpu.CompilerParams(vmem_limit_bytes=40 * 2**20),
        cost_estimate=pl.CostEstimate(
            flops=0, bytes_accessed=4 * count * rows * columns, transcendentals=0
        ),
    )(owners, *operands)


def spread(chunk, me, count):
    pieces = [(me, chunk)]
    stride = 2 if count % 2 == 0 else 1
    for hop in range(stride, count, stride):
        sent = lax.ppermute(chunk, "dp", [(i, (i + hop) % count) for i in range(count)])
        pieces.append((lax.rem(me - hop + count, count), sent))
    if stride == 2:
        swap = [(i, i ^ 1) for i in range(count)]
        for owner, piece in list(pieces):
            pieces.append((owner ^ 1, lax.ppermute(piece, "dp", swap)))
    return pieces


def on_device(
    activations,
    weight,
    readout,
    logp_rest,
    old_logp,
    ref_logp,
    lengths,
    group_ids,
    rewards,
    first_moment,
    second_moment,
):
    count = lax.axis_size("dp")
    me = lax.axis_index("dp")
    shard_rows = first_moment.shape[1]
    shifts = [[(i, (i + hop) % count) for i in range(count)] for hop in range(1, count)]

    gathered = lax.all_gather(activations, "section", axis=0, tiled=True)
    tok_rep = gathered.shape[0]
    tokens = count * tok_rep
    blocks = gathered.reshape(tok_rep, count, shard_rows)

    def block_for(owner):
        return lax.dynamic_index_in_dim(blocks, owner, axis=1, keepdims=False)

    left = [block_for(me)]
    right = [readout]
    for hop in range(1, count):
        left.append(lax.ppermute(block_for(lax.rem(me + hop, count)), "dp", shifts[hop - 1]))
        right.append(lax.ppermute(readout, "dp", shifts[hop - 1]))
    order = [lax.rem(me - hop + count, count) for hop in range(count)]

    layer_out = jnp.dot(gathered, weight, preferred_element_type=jnp.float32)
    score_share = jnp.sum(layer_out * readout.astype(jnp.float32), axis=1)
    first_holder = (lax.axis_index("section") + lax.axis_index("mp")) == 0
    once = jnp.where(first_holder, 1.0, 0.0).astype(jnp.float32)
    mine = jnp.stack([score_share + once * logp_rest, once * old_logp, once * ref_logp])
    slots = (jnp.arange(count) == me).astype(jnp.float32)
    known = lax.psum(mine[:, None, :] * slots[None, :, None], ("section", "dp", "mp"))
    known = known.reshape(3, tokens)
    positions = jnp.arange(tokens, dtype=jnp.int32)
    adv_token, token_weight = token_terms(lengths, group_ids, rewards, positions, RESP_LEN)
    coeff = token_coeff(known[0], known[1], known[2], adv_token, token_weight)
    coeff = coeff.reshape(count, tok_rep)
    coeff = jnp.concatenate(
        [lax.dynamic_index_in_dim(coeff, owner, axis=0, keepdims=False) for owner in order]
    )

    left = jnp.concatenate(left, axis=0).T
    right = jnp.concatenate(right, axis=0)
    weighted = (coeff[:, None] * right.astype(jnp.float32)).astype(jnp.bfloat16)

    chunks = max(n for n in range(1, 7) if shard_rows % (16 * n) == 0)
    rows = shard_rows // chunks
    tile = rows // 2 if rows % 32 == 0 else rows
    where_am_i = me.reshape(1).astype(jnp.int32)
    moments = new_weight = None
    sent, placed = [], []

    def place(chunk):
        pieces = sent[chunk]
        owners = jnp.stack([owner for owner, _ in pieces]).astype(jnp.int32)
        whole, token = place_rows(
            owners, [piece for _, piece in pieces], new_weight, shard_rows, chunk * rows
        )
        placed.append(token)
        return whole

    for chunk in range(chunks):
        if chunk >= 2:
            new_weight = place(chunk - 2)
        updated, *moments = update_rows(
            where_am_i,
            left,
            weighted,
            weight,
            first_moment[0],
            second_moment[0],
            moments,
            placed[-1] if placed else None,
            chunk * rows,
            rows,
            tile,
        )
        sent.append(spread(updated, me, count))
    for chunk in range(max(chunks - 2, 0), chunks):
        new_weight = place(chunk)
    return (new_weight, moments[0][None], moments[1][None])


def solution(mesh):
    placed = (
        P(("dp", "section"), "mp"),
        P("mp", "section"),
        P("dp", "section"),
        P("dp"),
        P("dp"),
        P("dp"),
        P(),
        P(),
        P(),
        P("mp", "dp", "section"),
        P("mp", "dp", "section"),
    )
    return jax.shard_map(
        on_device,
        mesh=mesh,
        in_specs=placed,
        out_specs=(P("mp", "section"), P("mp", "dp", "section"), P("mp", "dp", "section")),
        check_vma=False,
    )
```

```python
import functools

import jax
import jax.numpy as jnp
from jax import lax
from jax.experimental import pallas as pl
from jax.experimental.pallas import tpu as pltpu
from jax.sharding import PartitionSpec as P

RESP_LEN = 384


clip_eps = 0.2
kl_coef = 0.1
beta_one = 0.9
beta_two = 0.95
adam_eps = 1e-08
learn_rate = 0.0003
weight_decay = 0.1
first_correct = 1.0 - 0.9**10
second_correct = 1.0 - 0.95**10


def token_terms(lengths, group_ids, rewards, positions, resp_len):
    total_resp = rewards.shape[0]
    members = (group_ids[:, None] == group_ids[None, :]).astype(jnp.float32)
    group_size = jnp.sum(members, axis=1)
    group_mean = jnp.sum(members * rewards[None, :], axis=1) / group_size
    deviation = rewards[None, :] - group_mean[:, None]
    group_spread = jnp.sqrt(jnp.sum(members * deviation * deviation, axis=1) / group_size)
    advantage = (rewards - group_mean) / jnp.maximum(group_spread, 1.0)
    response = positions // resp_len
    slot_index = (positions % resp_len).astype(jnp.float32)
    picker = (response[:, None] == jnp.arange(total_resp, dtype=jnp.int32)[None, :]).astype(
        jnp.float32
    )
    adv_token = jnp.sum(picker * advantage[None, :], axis=1)
    len_token = jnp.sum(picker * lengths.astype(jnp.float32)[None, :], axis=1)
    token_weight = jnp.where(slot_index < len_token, 1.0 / (len_token * total_resp), 0.0)
    return (adv_token, token_weight)


def token_loss(new_logp, old_logp, ref_logp, adv_token, token_weight):
    ratio = jnp.exp(new_logp - old_logp)
    surrogate = jnp.minimum(
        ratio * adv_token, jnp.clip(ratio, 1.0 - clip_eps, 1.0 + clip_eps) * adv_token
    )
    gap = ref_logp - new_logp
    kl_term = jnp.exp(gap) - gap - 1.0
    return jnp.sum(token_weight * (kl_coef * kl_term - surrogate))


def token_coeff(new_logp, old_logp, ref_logp, adv_token, token_weight):

    def loss_of(values):
        return token_loss(values, old_logp, ref_logp, adv_token, token_weight)

    _, pullback = jax.vjp(loss_of, new_logp)
    return pullback(jnp.float32(1.0))[0]


def adam_rows(weight_rows, first_rows, second_rows, gradient):
    new_first = beta_one * first_rows + (1.0 - beta_one) * gradient
    new_second = beta_two * second_rows + (1.0 - beta_two) * gradient * gradient
    current = weight_rows.astype(jnp.float32)
    update = (
        new_first / first_correct / (jnp.sqrt(new_second / second_correct) + adam_eps)
        + weight_decay * current
    )
    return ((current - learn_rate * update).astype(jnp.bfloat16), new_first, new_second)


def update_kernel(count, place, *refs):
    weight, first, second = refs[2 * count : 2 * count + 3]
    updated, new_first, new_second = refs[-3:]
    gradient = jnp.dot(refs[0][...], refs[count][...], preferred_element_type=jnp.float32)
    for i in range(1, count):
        gradient += jnp.dot(
            refs[i][...], refs[count + i][...], preferred_element_type=jnp.float32
        )
    updated[...], new_first[...], new_second[...] = adam_rows(
        weight[...], first[...], second[...], gradient
    )


def update_rows(place, left, right, weight, first, second, carried, start, rows, tile):
    columns = weight.shape[1]
    count = len(left)
    tokens = right[0].shape[0]
    tiles = rows // tile
    begin = start // tile
    shard_tiles = first.shape[0] // tile
    here = lambda i, place: (begin + i, 0)
    moment = pl.BlockSpec((tile, columns), here)
    in_specs = [
        *[pl.BlockSpec((tile, tokens), here)] * count,
        *[pl.BlockSpec((tokens, columns), lambda i, place: (0, 0))] * count,
        pl.BlockSpec((tile, columns), lambda i, place: (place[0] * shard_tiles + begin + i, 0)),
        moment,
        moment,
    ]
    operands = [*left, *right, weight, first, second]
    aliases = {}
    if carried is not None:
        in_specs += [pl.BlockSpec(memory_space=pl.ANY)] * 2
        operands += list(carried)
        aliases = {2 * count + 4: 1, 2 * count + 5: 2}
    return pl.pallas_call(
        functools.partial(update_kernel, count),
        grid_spec=pltpu.PrefetchScalarGridSpec(
            num_scalar_prefetch=1,
            grid=(tiles,),
            in_specs=in_specs,
            out_specs=[pl.BlockSpec((tile, columns), lambda i, place: (i, 0)), moment, moment],
        ),
        out_shape=[
            jax.ShapeDtypeStruct((rows, columns), jnp.bfloat16),
            jax.ShapeDtypeStruct(first.shape, jnp.float32),
            jax.ShapeDtypeStruct(second.shape, jnp.float32),
        ],
        input_output_aliases=aliases,
        compiler_params=pltpu.CompilerParams(vmem_limit_bytes=40 * 2**20),
        cost_estimate=pl.CostEstimate(
            flops=2 * rows * count * tokens * columns,
            bytes_accessed=20 * rows * columns,
            transcendentals=rows * columns,
        ),
    )(place, *operands)


def place_kernel(count, shard_rows, start, owners, *rest):
    pieces = rest[:count]
    whole, token, held, in_sems, out_sems = rest[-5:]
    rows = pieces[0].shape[0]
    into = [
        pltpu.make_async_copy(pieces[i], held.at[i], in_sems.at[i]) for i in range(count)
    ]
    for copy in into:
        copy.start()
    token[...] = jnp.zeros_like(token)
    out = []
    for i in range(count):
        row = pl.multiple_of(owners[i] * shard_rows + start, 16)
        into[i].wait()
        out.append(pltpu.make_async_copy(held.at[i], whole.at[pl.ds(row, rows)], out_sems.at[i]))
        out[i].start()
    for copy in out:
        copy.wait()


def place_rows(owners, pieces, carried, shard_rows, start):
    count = len(pieces)
    rows, columns = pieces[0].shape
    anywhere = pl.BlockSpec(memory_space=pl.ANY)
    operands = list(pieces) + ([] if carried is None else [carried])
    return pl.pallas_call(
        functools.partial(place_kernel, count, shard_rows, start),
        in_specs=[pl.BlockSpec(memory_space=pltpu.SMEM)] + [anywhere] * len(operands),
        out_specs=[anywhere, pl.BlockSpec(memory_space=pltpu.VMEM)],
        out_shape=[
            jax.ShapeDtypeStruct((count * shard_rows, columns), jnp.bfloat16),
            jax.ShapeDtypeStruct((8, 128), jnp.float32),
        ],
        scratch_shapes=[
            pltpu.VMEM((count, rows, columns), jnp.bfloat16),
            pltpu.SemaphoreType.DMA((count,)),
            pltpu.SemaphoreType.DMA((count,)),
        ],
        input_output_aliases={} if carried is None else {count + 1: 0},
        compiler_params=pltpu.CompilerParams(vmem_limit_bytes=40 * 2**20),
        cost_estimate=pl.CostEstimate(
            flops=0, bytes_accessed=4 * count * rows * columns, transcendentals=0
        ),
    )(owners, *operands)


def gate_kernel(*refs):
    pass


def gate(piece, *tokens):
    anywhere = pl.BlockSpec(memory_space=pl.ANY)
    return pl.pallas_call(
        gate_kernel,
        in_specs=[anywhere] * (1 + len(tokens)),
        out_specs=anywhere,
        out_shape=jax.ShapeDtypeStruct(piece.shape, piece.dtype),
        input_output_aliases={0: 0},
    )(piece, *tokens)


def send_far(chunk, me, count):
    stride = 2 if count % 2 == 0 else 1
    far = []
    for hop in range(stride, count, stride):
        sent = lax.ppermute(chunk, "dp", [(i, (i + hop) % count) for i in range(count)])
        far.append((lax.rem(me - hop + count, count), sent))
    return far


def send_near(pieces, count):
    if count % 2:
        return pieces
    swap = [(i, i ^ 1) for i in range(count)]
    return pieces + [(owner ^ 1, lax.ppermute(piece, "dp", swap)) for owner, piece in pieces]


def on_device(
    activations,
    weight,
    readout,
    logp_rest,
    old_logp,
    ref_logp,
    lengths,
    group_ids,
    rewards,
    first_moment,
    second_moment,
):
    count = lax.axis_size("dp")
    me = lax.axis_index("dp")
    shard_rows = first_moment.shape[1]
    shifts = [[(i, (i + hop) % count) for i in range(count)] for hop in range(1, count)]

    sections = lax.axis_size("section")
    section = lax.axis_index("section")
    halves = [activations]
    for hop in range(1, sections):
        shift = [(i, (i + hop) % sections) for i in range(sections)]
        halves.append(lax.ppermute(activations, "section", shift))
    gathered = jnp.concatenate(
        [
            lax.select_n(lax.rem(section - j + sections, sections), *halves)
            for j in range(sections)
        ]
    )
    tok_rep = gathered.shape[0]
    turned = gathered.T

    def block_for(owner):
        return lax.dynamic_slice_in_dim(turned, owner * shard_rows, shard_rows, 0)

    left = [block_for(me)]
    right = [readout]
    for hop in range(1, count):
        left.append(lax.ppermute(block_for(lax.rem(me + hop, count)), "dp", shifts[hop - 1]))
        right.append(lax.ppermute(readout, "dp", shifts[hop - 1]))

    layer_out = jnp.dot(gathered, weight, preferred_element_type=jnp.float32)
    score_share = jnp.sum(layer_out * readout.astype(jnp.float32), axis=1)
    score_share = gate(score_share[None], *left)[0]
    new_logp = logp_rest + lax.psum(score_share, ("section", "mp"))
    positions = me * tok_rep + jnp.arange(tok_rep, dtype=jnp.int32)
    adv_token, token_weight = token_terms(lengths, group_ids, rewards, positions, RESP_LEN)
    coeff = token_coeff(new_logp, old_logp, ref_logp, adv_token, token_weight)
    coeffs = [coeff] + [lax.ppermute(coeff, "dp", shift) for shift in shifts]
    weighted = []
    for here, block in zip(coeffs, right):
        weighted.append((here[:, None] * block.astype(jnp.float32)).astype(jnp.bfloat16))

    chunks = max(n for n in range(1, 7) if shard_rows % (16 * n) == 0)
    rows = shard_rows // chunks
    tile = rows // 2 if rows % 32 == 0 else rows
    where_am_i = me.reshape(1).astype(jnp.int32)
    moments = new_weight = None
    sent, tokens = [], []
    for chunk in range(chunks):
        updated, *moments = update_rows(
            where_am_i,
            left,
            weighted,
            weight,
            first_moment[0],
            second_moment[0],
            moments,
            chunk * rows,
            rows,
            tile,
        )
        sent.append((updated, send_far(updated, me, count)))
    for chunk, (own, far) in enumerate(sent):
        if chunk == 1:
            far = [(owner, gate(piece, sent[-1][0])) for owner, piece in far]
        if chunk == chunks - 1 and chunk > 2:
            far = [(owner, gate(piece, tokens[chunk - 2])) for owner, piece in far]
        pieces = send_near([(me, own)] + far, count)
        owners = jnp.stack([owner for owner, _ in pieces]).astype(jnp.int32)
        new_weight, token = place_rows(
            owners, [piece for _, piece in pieces], new_weight, shard_rows, chunk * rows
        )
        tokens.append(token)
    return (new_weight, moments[0][None], moments[1][None])


def solution(mesh):
    placed = (
        P(("dp", "section"), "mp"),
        P("mp", "section"),
        P("dp", "section"),
        P("dp"),
        P("dp"),
        P("dp"),
        P(),
        P(),
        P(),
        P("mp", "dp", "section"),
        P("mp", "dp", "section"),
    )
    return jax.shard_map(
        on_device,
        mesh=mesh,
        in_specs=placed,
        out_specs=(P("mp", "section"), P("mp", "dp", "section"), P("mp", "dp", "section")),
        check_vma=False,
    )
```

```python
import functools

import jax
import jax.numpy as jnp
from jax import lax
from jax.experimental import pallas as pl
from jax.experimental.pallas import tpu as pltpu
from jax.sharding import PartitionSpec as P

RESP_LEN = 384


clip_eps = 0.2
kl_coef = 0.1
beta_one = 0.9
beta_two = 0.95
adam_eps = 1e-08
learn_rate = 0.0003
weight_decay = 0.1
first_correct = 1.0 - 0.9**10
second_correct = 1.0 - 0.95**10


def token_terms(lengths, group_ids, rewards, positions, resp_len):
    total_resp = rewards.shape[0]
    members = (group_ids[:, None] == group_ids[None, :]).astype(jnp.float32)
    group_size = jnp.sum(members, axis=1)
    group_mean = jnp.sum(members * rewards[None, :], axis=1) / group_size
    deviation = rewards[None, :] - group_mean[:, None]
    group_spread = jnp.sqrt(jnp.sum(members * deviation * deviation, axis=1) / group_size)
    advantage = (rewards - group_mean) / jnp.maximum(group_spread, 1.0)
    response = positions // resp_len
    slot_index = (positions % resp_len).astype(jnp.float32)
    picker = (response[:, None] == jnp.arange(total_resp, dtype=jnp.int32)[None, :]).astype(
        jnp.float32
    )
    adv_token = jnp.sum(picker * advantage[None, :], axis=1)
    len_token = jnp.sum(picker * lengths.astype(jnp.float32)[None, :], axis=1)
    token_weight = jnp.where(slot_index < len_token, 1.0 / (len_token * total_resp), 0.0)
    return (adv_token, token_weight)


def token_loss(new_logp, old_logp, ref_logp, adv_token, token_weight):
    ratio = jnp.exp(new_logp - old_logp)
    surrogate = jnp.minimum(
        ratio * adv_token, jnp.clip(ratio, 1.0 - clip_eps, 1.0 + clip_eps) * adv_token
    )
    gap = ref_logp - new_logp
    kl_term = jnp.exp(gap) - gap - 1.0
    return jnp.sum(token_weight * (kl_coef * kl_term - surrogate))


def token_coeff(new_logp, old_logp, ref_logp, adv_token, token_weight):

    def loss_of(values):
        return token_loss(values, old_logp, ref_logp, adv_token, token_weight)

    _, pullback = jax.vjp(loss_of, new_logp)
    return pullback(jnp.float32(1.0))[0]


def adam_rows(weight_rows, first_rows, second_rows, gradient):
    new_first = beta_one * first_rows + (1.0 - beta_one) * gradient
    new_second = beta_two * second_rows + (1.0 - beta_two) * gradient * gradient
    current = weight_rows.astype(jnp.float32)
    update = (
        new_first / first_correct / (jnp.sqrt(new_second / second_correct) + adam_eps)
        + weight_decay * current
    )
    return ((current - learn_rate * update).astype(jnp.bfloat16), new_first, new_second)


def update_kernel(count, place, *refs):
    weight, first, second = refs[2 * count : 2 * count + 3]
    updated, new_first, new_second = refs[-3:]
    gradient = jnp.dot(refs[0][...], refs[count][...], preferred_element_type=jnp.float32)
    for i in range(1, count):
        gradient += jnp.dot(
            refs[i][...], refs[count + i][...], preferred_element_type=jnp.float32
        )
    updated[...], new_first[...], new_second[...] = adam_rows(
        weight[...], first[...], second[...], gradient
    )


def update_rows(place, left, right, weight, first, second, carried, start, rows, tile):
    columns = weight.shape[1]
    count = len(left)
    tokens = right[0].shape[0]
    tiles = rows // tile
    begin = start // tile
    shard_tiles = first.shape[0] // tile
    here = lambda i, place: (begin + i, 0)
    moment = pl.BlockSpec((tile, columns), here)
    in_specs = [
        *[pl.BlockSpec((tile, tokens), here)] * count,
        *[pl.BlockSpec((tokens, columns), lambda i, place: (0, 0))] * count,
        pl.BlockSpec((tile, columns), lambda i, place: (place[0] * shard_tiles + begin + i, 0)),
        moment,
        moment,
    ]
    operands = [*left, *right, weight, first, second]
    aliases = {}
    if carried is not None:
        in_specs += [pl.BlockSpec(memory_space=pl.ANY)] * 2
        operands += list(carried)
        aliases = {2 * count + 4: 1, 2 * count + 5: 2}
    return pl.pallas_call(
        functools.partial(update_kernel, count),
        grid_spec=pltpu.PrefetchScalarGridSpec(
            num_scalar_prefetch=1,
            grid=(tiles,),
            in_specs=in_specs,
            out_specs=[pl.BlockSpec((tile, columns), lambda i, place: (i, 0)), moment, moment],
        ),
        out_shape=[
            jax.ShapeDtypeStruct((rows, columns), jnp.bfloat16),
            jax.ShapeDtypeStruct(first.shape, jnp.float32),
            jax.ShapeDtypeStruct(second.shape, jnp.float32),
        ],
        input_output_aliases=aliases,
        compiler_params=pltpu.CompilerParams(vmem_limit_bytes=40 * 2**20),
        cost_estimate=pl.CostEstimate(
            flops=2 * rows * count * tokens * columns,
            bytes_accessed=20 * rows * columns,
            transcendentals=rows * columns,
        ),
    )(place, *operands)


def place_kernel(count, shard_rows, start, owners, *rest):
    pieces = rest[:count]
    whole, token, held, in_sems, out_sems = rest[-5:]
    rows = pieces[0].shape[0]
    into = [
        pltpu.make_async_copy(pieces[i], held.at[i], in_sems.at[i]) for i in range(count)
    ]
    for copy in into:
        copy.start()
    token[...] = jnp.zeros_like(token)
    out = []
    for i in range(count):
        row = pl.multiple_of(owners[i] * shard_rows + start, 16)
        into[i].wait()
        out.append(pltpu.make_async_copy(held.at[i], whole.at[pl.ds(row, rows)], out_sems.at[i]))
        out[i].start()
    for copy in out:
        copy.wait()


def place_rows(owners, pieces, carried, shard_rows, start):
    count = len(pieces)
    rows, columns = pieces[0].shape
    anywhere = pl.BlockSpec(memory_space=pl.ANY)
    operands = list(pieces) + ([] if carried is None else [carried])
    return pl.pallas_call(
        functools.partial(place_kernel, count, shard_rows, start),
        in_specs=[pl.BlockSpec(memory_space=pltpu.SMEM)] + [anywhere] * len(operands),
        out_specs=[anywhere, pl.BlockSpec(memory_space=pltpu.VMEM)],
        out_shape=[
            jax.ShapeDtypeStruct((count * shard_rows, columns), jnp.bfloat16),
            jax.ShapeDtypeStruct((8, 128), jnp.float32),
        ],
        scratch_shapes=[
            pltpu.VMEM((count, rows, columns), jnp.bfloat16),
            pltpu.SemaphoreType.DMA((count,)),
            pltpu.SemaphoreType.DMA((count,)),
        ],
        input_output_aliases={} if carried is None else {count + 1: 0},
        compiler_params=pltpu.CompilerParams(vmem_limit_bytes=40 * 2**20),
        cost_estimate=pl.CostEstimate(
            flops=0, bytes_accessed=4 * count * rows * columns, transcendentals=0
        ),
    )(owners, *operands)


def gate_kernel(*refs):
    pass


def gate(piece, *tokens):
    anywhere = pl.BlockSpec(memory_space=pl.ANY)
    return pl.pallas_call(
        gate_kernel,
        in_specs=[anywhere] * (1 + len(tokens)),
        out_specs=anywhere,
        out_shape=jax.ShapeDtypeStruct(piece.shape, piece.dtype),
        input_output_aliases={0: 0},
    )(piece, *tokens)


def send_far(chunk, me, count):
    stride = 2 if count % 2 == 0 else 1
    far = []
    for hop in range(stride, count, stride):
        sent = lax.ppermute(chunk, "dp", [(i, (i + hop) % count) for i in range(count)])
        far.append((lax.rem(me - hop + count, count), sent))
    return far


def send_near(pieces, count):
    if count % 2:
        return pieces
    swap = [(i, i ^ 1) for i in range(count)]
    return pieces + [(owner ^ 1, lax.ppermute(piece, "dp", swap)) for owner, piece in pieces]


def on_device(
    activations,
    weight,
    readout,
    logp_rest,
    old_logp,
    ref_logp,
    lengths,
    group_ids,
    rewards,
    first_moment,
    second_moment,
):
    count = lax.axis_size("dp")
    me = lax.axis_index("dp")
    shard_rows = first_moment.shape[1]
    shifts = [[(i, (i + hop) % count) for i in range(count)] for hop in range(1, count)]

    sections = lax.axis_size("section")
    section = lax.axis_index("section")
    halves = [activations]
    for hop in range(1, sections):
        shift = [(i, (i + hop) % sections) for i in range(sections)]
        halves.append(lax.ppermute(activations, "section", shift))
    gathered = jnp.concatenate(
        [
            lax.select_n(lax.rem(section - j + sections, sections), *halves)
            for j in range(sections)
        ]
    )
    tok_rep = gathered.shape[0]
    turned = gathered.T

    def block_for(owner):
        return lax.dynamic_slice_in_dim(turned, owner * shard_rows, shard_rows, 0)

    left = [block_for(me)]
    right = [readout]
    for hop in range(1, count):
        left.append(lax.ppermute(block_for(lax.rem(me + hop, count)), "dp", shifts[hop - 1]))
        right.append(lax.ppermute(readout, "dp", shifts[hop - 1]))

    layer_out = jnp.dot(gathered, weight, preferred_element_type=jnp.float32)
    score_share = jnp.sum(layer_out * readout.astype(jnp.float32), axis=1)
    score_share = gate(score_share[None], *left)[0]
    new_logp = logp_rest + lax.psum(score_share, ("section", "mp"))
    positions = me * tok_rep + jnp.arange(tok_rep, dtype=jnp.int32)
    adv_token, token_weight = token_terms(lengths, group_ids, rewards, positions, RESP_LEN)
    coeff = token_coeff(new_logp, old_logp, ref_logp, adv_token, token_weight)
    coeffs = [coeff] + [lax.ppermute(coeff, "dp", shift) for shift in shifts]
    weighted = []
    for here, block in zip(coeffs, right):
        weighted.append((here[:, None] * block.astype(jnp.float32)).astype(jnp.bfloat16))

    chunks = max(n for n in range(1, 10) if shard_rows % (16 * n) == 0)
    rows = shard_rows // chunks
    tile = rows // 2 if rows % 32 == 0 else rows
    where_am_i = me.reshape(1).astype(jnp.int32)
    moments = new_weight = None
    sent, tokens = [], []
    for chunk in range(chunks):
        updated, *moments = update_rows(
            where_am_i,
            left,
            weighted,
            weight,
            first_moment[0],
            second_moment[0],
            moments,
            chunk * rows,
            rows,
            tile,
        )
        sent.append((updated, send_far(updated, me, count)))
    for chunk, (own, far) in enumerate(sent):
        if chunk == 1:
            far = [(owner, gate(piece, sent[-1][0])) for owner, piece in far]
        if chunk == chunks - 1 and chunk > 2:
            far = [(owner, gate(piece, tokens[chunk - 2])) for owner, piece in far]
        pieces = send_near([(me, own)] + far, count)
        owners = jnp.stack([owner for owner, _ in pieces]).astype(jnp.int32)
        new_weight, token = place_rows(
            owners, [piece for _, piece in pieces], new_weight, shard_rows, chunk * rows
        )
        tokens.append(token)
    return (new_weight, moments[0][None], moments[1][None])


def solution(mesh):
    placed = (
        P(("dp", "section"), "mp"),
        P("mp", "section"),
        P("dp", "section"),
        P("dp"),
        P("dp"),
        P("dp"),
        P(),
        P(),
        P(),
        P("mp", "dp", "section"),
        P("mp", "dp", "section"),
    )
    return jax.shard_map(
        on_device,
        mesh=mesh,
        in_specs=placed,
        out_specs=(P("mp", "section"), P("mp", "dp", "section"), P("mp", "dp", "section")),
        check_vma=False,
    )
```
